256 devices in a mesh: row: 16 (over x, y), col: 16 (over z, core).
Axes of the slice: x: 4, y: 4, z: 8, core: 2. Of those that a mesh axis runs over, the one named last changes fastest.
Arguments:
- matrix_cyclic: float32 [16384, 16384], P('row', 'col'), as said below
Outputs:
- reduced: float32 [16384, 16384], P('row', 'col')
- band_factors: float32 [2, 256, 256], replicated
Inputs may be any that keep to these rules, and one draw needn't show every extreme that they name: `matrix_cyclic`: in global order the matrix is symmetric up to rounding.
All inputs are finite; a program needn't handle non-finite values.
Results may differ from the reference program's by a relative error of at most 0.00016.
Values sent between devices are 32-bit elements; how exact they have to be, the bound alone decides.
A program may use at most 128 MiB of HBM per device.

```python
import jax
import jax.numpy as jnp
from jax import lax

PANEL = 256
N = 16384
N_ROW = 16
N_COL = 16


def draw_matrix_cyclic(key, part):
    order = N
    base = jnp.clip(jax.random.normal(key, (order, order), jnp.float32), -4.0, 4.0)
    full = (base + base.T) * 0.7071067811865476
    row_blocks = order // (PANEL * N_ROW)
    col_blocks = order // (PANEL * N_COL)
    stored = full.reshape(row_blocks, N_ROW, PANEL, col_blocks, N_COL, PANEL)
    return stored.transpose(1, 0, 2, 4, 3, 5).reshape(order, order)


def setup_inputs(seed: int = 0) -> dict:
    arg_keys = jax.random.split(jax.random.key(seed), 2)
    matrix_cyclic = draw_matrix_cyclic(jax.random.fold_in(arg_keys[1], 71), 0)
    return dict(matrix_cyclic=matrix_cyclic)


def matmul(left, right):
    return jnp.dot(left.astype(jnp.float32), right.astype(jnp.float32), precision=lax.Precision.HIGHEST, preferred_element_type=jnp.float32)

def invert_near_identity(operand):
    identity = jnp.eye(operand.shape[0], dtype=jnp.float32)
    estimate = identity
    for iteration in range(6):
        estimate = matmul(estimate, 2.0 * identity - matmul(operand, estimate))
    return estimate

def reference(matrix_cyclic):
    width = PANEL
    order = N
    row_blocks = order // (width * N_ROW)
    col_blocks = order // (width * N_COL)
    full = matrix_cyclic.reshape(N_ROW, row_blocks, width, N_COL, col_blocks, width)
    full = full.transpose(1, 0, 2, 4, 3, 5).reshape(order, order)
    identity = jnp.eye(width, dtype=jnp.float32)
    uppers = []
    for panel_index in range(2):
        start = (panel_index + 1) * width
        panel = full[start:, panel_index * width:start]
        lower_factor = jnp.linalg.cholesky(matmul(panel.T, panel))
        q_rows = jax.scipy.linalg.solve_triangular(lower_factor, panel.T, lower=True).T
        q_top = q_rows[:width]
        inverse_t = invert_near_identity(identity - q_top.T)
        w_live = (-q_rows).at[:width].add(identity)
        w_full = jnp.concatenate([jnp.zeros((start, width), jnp.float32), w_live], axis=0)
        x_full = matmul(full, w_full)
        middle = matmul(w_full.T, x_full)
        sym_block = matmul(matmul(inverse_t.T, middle), inverse_t)
        u_full = matmul(x_full, inverse_t) - 0.5 * matmul(w_full, sym_block)
        left = jnp.concatenate([w_full, u_full], axis=1)
        right = jnp.concatenate([u_full, w_full], axis=1)
        full = full - matmul(left, right.T)
        uppers.append(lower_factor.T)
    keep = (jnp.arange(order) >= 2 * width).astype(jnp.float32)
    full = full * keep[:, None] * keep[None, :]
    stored = full.reshape(row_blocks, N_ROW, width, col_blocks, N_COL, width)
    stored = stored.transpose(1, 0, 2, 4, 3, 5).reshape(order, order)
    band = jnp.stack(uppers) / jnp.sqrt(jnp.float32(order))
    return (stored, band)
```

```python
import functools
import math

import jax
import jax.numpy as jnp
from jax import lax
from jax.experimental import pallas as pl
from jax.experimental.pallas import tpu as pltpu
from jax.sharding import PartitionSpec as P

B = 256
F32 = jnp.float32
HIGH = lax.Precision.HIGH
HIGHEST = lax.Precision.HIGHEST
NN = (((1,), (0,)), ((), ()))
NT = (((1,), (1,)), ((), ()))
TN = (((0,), (0,)), ((), ()))


def dot(left, right, dims=NN, precision=HIGH):
    return lax.dot_general(left, right, dims, precision=precision, preferred_element_type=F32)


class Place:
    def __init__(self):
        self.row = lax.axis_index("row")
        self.col = lax.axis_index("col")
        self.x, self.y = self.row // 4, lax.rem(self.row, 4)
        self.z, self.core = self.col // 2, lax.rem(self.col, 2)
        self.slot = self.core * 8 + self.z

    def z_peer(self, d):
        return (self.row, lax.rem(self.z + d, 8) * 2 + self.core)

    def z_slot_to(self, d):
        return self.core * 8 + lax.rem(self.z + d, 8)

    def z_slot_from(self, d):
        return self.core * 8 + lax.rem(self.z + 8 - d, 8)

    def sibling(self):
        return (self.row, self.col + 1 - 2 * self.core)

    def col_peer(self, t):
        return (self.row, lax.rem(self.col + t, 16))

    def col_slot_to(self, t):
        other = lax.rem(self.col + t, 16)
        return lax.rem(other, 2) * 8 + other // 2

    def row_peer(self, d):
        return (self.row_to(d), self.col)

    def row_to(self, d):
        return lax.rem(self.x + d // 4, 4) * 4 + lax.rem(self.y + lax.rem(d, 4), 4)

    def row_from(self, d):
        return lax.rem(self.x + 4 - d // 4, 4) * 4 + lax.rem(self.y + 4 - lax.rem(d, 4), 4)


def loop(start, stop, body):
    def step(i, carry):
        body(i)
        return carry

    lax.fori_loop(start, stop, step, 0)


class Comm:
    def __init__(self, place, send, recv):
        self.at = place
        self.send = send
        self.recv = recv
        self.used = 0
        self.sent = []

    def take(self, count):
        base = self.used
        self.used += count
        return base

    def copy(self, src, dst, send_index, recv_index, device):
        return pltpu.make_async_remote_copy(
            src_ref=src,
            dst_ref=dst,
            send_sem=self.send.at[send_index],
            recv_sem=self.recv.at[recv_index],
            device_id=device,
            device_id_type=pl.DeviceIdType.MESH,
        )

    def finish(self):
        for wait in self.sent:
            wait()


class Exchange:
    def __init__(self, comm, first, stop, peer, src, dst, landed):
        self.comm, self.first, self.stop = comm, first, stop
        self.peer, self.src, self.dst, self.landed = peer, src, dst, landed
        self.base = comm.take(stop - first) - first
        comm.sent.append(self.wait_sends)

    def start_one(self, d):
        i = self.base + d
        self.comm.copy(self.src(d), self.dst(d), i, i, self.peer(d)).start()

    def start(self):
        loop(self.first, self.stop, self.start_one)

    def wait_one(self, d):
        i = self.base + d
        self.comm.copy(self.landed(d), self.landed(d), i, i, self.peer(d)).wait_recv()

    def wait(self):
        loop(self.first, self.stop, self.wait_one)

    def wait_sends(self):
        def one(d):
            i = self.base + d
            self.comm.copy(self.src(d), self.dst(d), i, i, self.peer(d)).wait_send()

        loop(self.first, self.stop, one)


class Deal:
    def __init__(self, comm, source, peer, src, dst, landed):
        self.comm, self.source = comm, source
        self.peer, self.src, self.dst, self.landed = peer, src, dst, landed
        self.base = comm.take(16)
        comm.sent.append(self.wait_sends)

    def copy(self, t):
        return self.comm.copy(self.src(t), self.dst(t), self.base + t, self.base, self.peer(t))

    def start(self):
        @pl.when(self.source)
        def _():
            loop(1, 16, lambda t: self.copy(t).start())

    def wait(self):
        @pl.when(jnp.logical_not(self.source))
        def _():
            self.comm.copy(self.landed, self.landed, self.base, self.base, self.peer(1)).wait_recv()

    def wait_sends(self):
        @pl.when(self.source)
        def _():
            loop(1, 16, lambda t: self.copy(t).wait_send())


class GatherCol:
    def __init__(self, comm, part):
        at = comm.at
        self.at = at
        self.z = Exchange(
            comm, 1, 8, at.z_peer, lambda d: part(at.slot), lambda d: part(at.slot), lambda d: part(at.z_slot_from(d))
        )
        sibling = lambda d: at.sibling()
        other = lambda d: (1 - at.core) * 8 + lax.rem(at.z + 8 - d, 8)
        self.pair = Exchange(
            comm, 0, 8, sibling, lambda d: part(at.z_slot_from(d)), lambda d: part(at.z_slot_from(d)),
            lambda d: part(other(d)),
        )

    def start(self):
        self.z.start()
        self.pair.start_one(0)

    def forward(self):
        def one(d):
            self.z.wait_one(d)
            self.pair.start_one(d)

        loop(1, 8, one)

    def wait(self):
        self.pair.wait()


def cholesky_strips(aug, first, stop):
    sub = lax.broadcasted_iota(jnp.int32, (8, 128), 0)
    lane = lax.broadcasted_iota(jnp.int32, (8, B), 1)

    def strip(s):
        rows = pl.ds(pl.multiple_of(8 * s, 8), 8)
        diag = aug[rows, pl.ds(pl.multiple_of((s // 16) * 128, 128), 128)]
        diag = pltpu.roll(diag, lax.rem(128 - 8 * lax.rem(s, 16), 128), 1)
        parts = [aug[rows, 128 * k : 128 * k + 128] for k in range(4)]
        cols = [jnp.broadcast_to(diag[:, j : j + 1], (8, 128)) for j in range(8)]
        pivots = jnp.ones((8, 128), F32)
        for j in range(8):
            pivot = jnp.broadcast_to(cols[j][j : j + 1, :], (8, 128))
            pivots = jnp.where(sub == j, pivot, pivots)
            scale = jnp.where(sub > j, cols[j] / pivot, 0.0)
            for k in range(j + 1, 8):
                cols[k] = cols[k] - scale * jnp.broadcast_to(cols[k][j : j + 1, :], (8, 128))
            for k in range(4):
                parts[k] = parts[k] - scale * jnp.broadcast_to(parts[k][j : j + 1, :], (8, 128))
        norm = 1.0 / jnp.sqrt(pivots)
        parts = [part * norm for part in parts]
        whole = jnp.concatenate(parts, axis=1)
        left = jnp.where(lane >= 8 * (s + 1), whole[:, :B], 0.0)
        aug[...] = aug[...] - dot(left.T, whole, NN, HIGHEST)
        aug[rows, :] = whole

    loop(first, stop, strip)


def kernel(a_ref, out_ref, band_ref, g, stage_r, stage_c, pr, pc, er, ec, prt, ypr, ypc, half, zr, xr, yr, yc,
           gx, sm1, sm2, aug, left, right, small, local_sem, send_sem, recv_sem):
    at = Place()
    comm = Comm(at, send_sem, recv_sem)
    row, col, slot = at.row, at.col, at.slot
    load = pltpu.make_async_copy(a_ref, g, local_sem.at[0])
    load.start()
    barrier = pltpu.get_barrier_semaphore()

    def greet(t):
        pl.semaphore_signal(barrier, inc=1, device_id=at.col_peer(t), device_id_type=pl.DeviceIdType.MESH)
        pl.semaphore_signal(barrier, inc=1, device_id=at.row_peer(t), device_id_type=pl.DeviceIdType.MESH)

    loop(1, 16, greet)
    load.wait()
    pl.semaphore_wait(barrier, 30)

    def rows64(ref, s):
        return ref.at[pl.ds(pl.multiple_of(64 * s, 64), 64)]

    def rows16(ref, s):
        return ref.at[pl.ds(pl.multiple_of(16 * s, 16), 16)]

    class Spread:
        def __init__(self, b, to_r, to_c):
            self.b, self.to_r, self.to_c = b, to_r, to_c
            self.deal_r = Deal(
                comm, col == b, at.col_peer,
                lambda t: rows64(stage_r, at.col_slot_to(t)), lambda t: rows64(to_r, at.col_slot_to(t)),
                rows64(to_r, slot),
            )
            self.deal_c = Deal(
                comm, row == b, at.row_peer,
                lambda t: rows16(stage_c, at.row_to(t)), lambda t: rows16(to_c, at.row_to(t)), rows16(to_c, row),
            )
            self.gather_r = GatherCol(comm, lambda s: rows64(to_r, s))
            self.gather_c = Exchange(
                comm, 1, 16, at.row_peer, lambda d: rows16(to_c, row), lambda d: rows16(to_c, row),
                lambda d: rows16(to_c, at.row_from(d)),
            )

        def deal(self, masked):
            @pl.when(col == self.b)
            def _():
                stage_r[...] = g[:, 0:B]
                if masked:
                    @pl.when(row == 0)
                    def _():
                        stage_r[0:B, :] = jnp.zeros((B, B), F32)
                mine = pl.ds(pl.multiple_of(64 * slot, 64), 64)
                self.to_r[mine, :] = stage_r[mine, :]

            self.deal_r.start()

            @pl.when(row == self.b)
            def _():
                stage_c[...] = g[0:B, :]
                if masked:
                    @pl.when(col == 0)
                    def _():
                        stage_c[:, 0:B] = jnp.zeros((B, B), F32)
                mine = pl.ds(pl.multiple_of(16 * row, 16), 16)
                self.to_c[mine, :] = stage_c[mine, :]

            self.deal_c.start()

        def gather(self):
            self.deal_r.wait()
            self.gather_r.start()
            self.deal_c.wait()
            self.gather_c.start()

        def forward(self):
            self.gather_r.forward()

        def wait(self):
            self.gather_r.wait()
            self.gather_c.wait()

    def panel(p, spread_e):
        panel_r, panel_c, side_r, side_c = pr.at[p], pc.at[p], er.at[p], ec.at[p]
        top = p + 1
        sums1, sums2, full_r, full_c = sm1.at[p], sm2.at[p], yr.at[p], yc.at[p]
        mine16 = pl.ds(pl.multiple_of(16 * slot, 16), 16)

        def small_sum(which, sums, value, rows):
            own, got = gx.at[p, which, 0], gx.at[p, which]
            own[...] = value
            ring = Exchange(comm, 1, 16, at.row_peer, lambda d: own, lambda d: got.at[d], lambda d: got.at[d])
            ring.start()
            tops = sums.at[slot, pl.ds(16, rows - 16)]
            deal = Deal(comm, row == top, at.row_peer, lambda t: tops, lambda t: tops, tops)
            gather = GatherCol(comm, lambda s: sums.at[s])
            return ring, got, deal, gather

        def small_finish(parts, sums):
            ring, got, deal, gather = parts
            ring.wait()
            total = got[0]
            for d in range(1, 16):
                total = total + got[d]
            sums[slot, 0:16, :] = total
            deal.wait()
            gather.start()

        prt[...] = panel_r[...].T
        gram_parts = small_sum(0, sums1, dot(prt[mine16, :], panel_r[...], NN, HIGHEST), 32)

        @pl.when(row == top)
        def _():
            sums1[slot, 16:32, :] = panel_r[mine16, :]

        gram_parts[2].start()

        if p == 1:
            def update(n):
                lanes = pl.ds(pl.multiple_of(n * B, B), B)
                g[:, lanes] = g[:, lanes] - dot(left[...], right[:, lanes])

            loop(0, 4, update)
            spread_e.deal(False)

        pair = Exchange(
            comm, 0, 1, lambda d: at.sibling(),
            lambda d: ypr.at[p, pl.ds(pl.multiple_of(512 * (1 - at.core), 512), 512)], lambda d: half.at[p],
            lambda d: half.at[p],
        )
        cross = Exchange(
            comm, 1, 8, at.z_peer, lambda d: rows64(ypr.at[p], at.z_slot_to(d)), lambda d: zr.at[p, d],
            lambda d: zr.at[p, d],
        )
        ring = Exchange(
            comm, 1, 16, at.row_peer, lambda d: rows16(ypc.at[p], at.row_to(d)), lambda d: xr.at[p, d],
            lambda d: xr.at[p, d],
        )

        def product_rows(base, m):
            rows = pl.ds(pl.multiple_of(base + m * B, B), B)
            ypr[p, rows, :] = dot(g[rows, :], panel_c[...], NT)

        def product_cols(n):
            lanes = pl.ds(pl.multiple_of(n * B, B), B)
            ypc[p, :, lanes] = dot(prt[...], g[:, lanes])

        loop(0, 2, lambda m: product_rows(512 * (1 - at.core), m))
        pair.start()
        loop(0, 2, lambda m: product_rows(512 * at.core, m))
        pair.wait()
        mine512 = pl.ds(pl.multiple_of(512 * at.core, 512), 512)
        ypr[p, mine512, :] = ypr[p, mine512, :] + half[p]
        cross.start()
        loop(0, 4, product_cols)
        ring.start()

        small_finish(gram_parts, sums1)
        if p == 1:
            spread_e.gather()
        else:
            spread_e.forward()
        gram_parts[3].forward()
        gram_parts[3].wait()

        eye = (lax.broadcasted_iota(jnp.int32, (B, B), 0) == lax.broadcasted_iota(jnp.int32, (B, B), 1)).astype(F32)
        aug[:, 0:B] = sums1[:, 0:16, :].reshape(B, B)
        aug[:, B : 2 * B] = eye
        cholesky_strips(aug, 0, 16)

        cross.wait()
        mine64 = pl.ds(pl.multiple_of(64 * slot, 64), 64)
        total = ypr[p, mine64, :]
        for d in range(1, 8):
            total = total + zr[p, d]
        full_r[mine64, :] = total
        gather_r = GatherCol(comm, lambda s: rows64(full_r, s))
        gather_r.start()
        ring.wait()
        own16 = pl.ds(pl.multiple_of(16 * row, 16), 16)
        total = ypc[p, own16, :]
        for d in range(1, 16):
            total = total + xr[p, d]
        full_c[own16, :] = total
        gather_c = Exchange(
            comm, 1, 16, at.row_peer, lambda d: rows16(full_c, row), lambda d: rows16(full_c, row),
            lambda d: rows16(full_c, at.row_from(d)),
        )
        gather_c.start()

        cholesky_strips(aug, 16, 32)
        upper = jnp.where(
            lax.broadcasted_iota(jnp.int32, (B, B), 1) >= lax.broadcasted_iota(jnp.int32, (B, B), 0), aug[:, 0:B], 0.0
        )
        band_ref[p] = upper / 128.0
        inverse = aug[:, B : 2 * B]
        panel_top = sums1[:, 16:32, :].reshape(B, B)
        c_top = dot(panel_top, inverse, NT, HIGHEST)
        power = dot(inverse, panel_top, NT, HIGHEST)
        inverse_t = eye + power
        for _ in range(5):
            power = dot(power, power, NN, HIGHEST)
            inverse_t = inverse_t + dot(inverse_t, power, NN, HIGHEST)

        if p == 1:
            spread_e.forward()
        gather_r.forward()
        gather_r.wait()
        middle_parts = small_sum(1, sums2, dot(prt[mine16, :], full_r[...], NN, HIGHEST), 48)
        spread_e.wait()

        @pl.when(row == top)
        def _():
            sums2[slot, 16:32, :] = full_r[mine16, :]
            sums2[slot, 32:48, :] = side_r[mine16, :]

        middle_parts[2].start()

        def w_and_x_rows(m):
            rows = pl.ds(pl.multiple_of(m * B, B), B)
            left[rows, 0:B] = -dot(panel_r[rows, :], inverse, NT)
            left[rows, B : 2 * B] = dot(side_r[rows, :] - dot(full_r[rows, :], inverse, NT), inverse_t)

        loop(0, 4, w_and_x_rows)

        @pl.when(row == top)
        def _():
            left[0:B, 0:B] = left[0:B, 0:B] + eye

        gather_c.wait()

        def w_and_x_cols(n):
            lanes = pl.ds(pl.multiple_of(n * B, B), B)
            right[B : 2 * B, lanes] = -dot(inverse, panel_c[:, lanes])
            right[0:B, lanes] = dot(inverse_t, side_c[:, lanes] - dot(inverse, full_c[:, lanes]), TN)

        loop(0, 4, w_and_x_cols)

        @pl.when(col == top)
        def _():
            right[B : 2 * B, 0:B] = right[B : 2 * B, 0:B] + eye

        small_finish(middle_parts, sums2)
        middle_parts[3].forward()
        middle_parts[3].wait()
        inner = sums2[:, 0:16, :].reshape(B, B)
        y_top = sums2[:, 16:32, :].reshape(B, B)
        e_top = sums2[:, 32:48, :].reshape(B, B)
        middle = (
            e_top
            - dot(y_top, inverse, NT, HIGHEST)
            - dot(inverse, y_top, NT, HIGHEST)
            + dot(dot(inverse, inner, NN, HIGHEST), inverse, NT, HIGHEST)
        )
        sym = dot(inverse_t, dot(middle, inverse_t, NN, HIGHEST), TN, HIGHEST)
        half_sym = 0.5 * sym

        def u_rows(m):
            rows = pl.ds(pl.multiple_of(m * B, B), B)
            left[rows, B : 2 * B] = left[rows, B : 2 * B] - dot(left[rows, 0:B], half_sym)

        loop(0, 4, u_rows)

        def u_cols(n):
            lanes = pl.ds(pl.multiple_of(n * B, B), B)
            right[0:B, lanes] = right[0:B, lanes] - dot(half_sym, right[B : 2 * B, lanes], TN)

        loop(0, 4, u_cols)
        if p == 1:
            return
        w_top = eye - c_top
        x_top = e_top - dot(y_top, inverse, NT, HIGHEST)
        u_top = dot(x_top, inverse_t, NN, HIGHEST) - dot(w_top, half_sym, NN, HIGHEST)
        small[0] = w_top
        small[1] = u_top

        def next_rows(m):
            rows = pl.ds(pl.multiple_of(m * B, B), B)
            pr[1, rows, :] = (
                side_r[rows, :]
                - dot(left[rows, 0:B], small[1], NT)
                - dot(left[rows, B : 2 * B], small[0], NT)
            )

        loop(0, 4, next_rows)

        @pl.when(row < 2)
        def _():
            pr[1, 0:B, :] = jnp.zeros((B, B), F32)

        def next_cols(n):
            lanes = pl.ds(pl.multiple_of(n * B, B), B)
            pc[1, :, lanes] = (
                side_c[:, lanes] - dot(small[1], right[B : 2 * B, lanes]) - dot(small[0], right[0:B, lanes])
            )

        loop(0, 4, next_cols)

        @pl.when(col < 2)
        def _():
            pc[1, :, 0:B] = jnp.zeros((B, B), F32)

    spread_p = Spread(0, pr.at[0], pc.at[0])
    spread_e = Spread(1, er.at[0], ec.at[0])
    spread_p.deal(True)
    spread_e.deal(False)
    spread_p.gather()
    spread_e.gather()
    spread_p.forward()
    spread_p.wait()
    panel(0, spread_e)
    panel(1, Spread(2, er.at[1], ec.at[1]))

    def last(n):
        lanes = pl.ds(pl.multiple_of(n * B, B), B)
        g[:, lanes] = g[:, lanes] - dot(left[...], right[:, lanes])

        @pl.when(row < 2)
        def _():
            g[0:B, lanes] = jnp.zeros((B, B), F32)

        @pl.when(jnp.logical_and(col < 2, n == 0))
        def _():
            g[:, lanes] = jnp.zeros((4 * B, B), F32)

        pltpu.make_async_copy(g.at[:, lanes], out_ref.at[:, lanes], local_sem.at[n]).start()

    loop(0, 4, last)
    comm.finish()

    def drain(n):
        lanes = pl.ds(pl.multiple_of(n * B, B), B)
        pltpu.make_async_copy(g.at[:, lanes], out_ref.at[:, lanes], local_sem.at[n]).wait()

    loop(0, 4, drain)


def shards(matrix_cyclic):
    vmem = lambda *shape: pltpu.VMEM(shape, F32)
    return pl.pallas_call(
        kernel,
        out_shape=(
            jax.ShapeDtypeStruct((1024, 1024), F32),
            jax.ShapeDtypeStruct((2, B, B), F32),
        ),
        in_specs=[pl.BlockSpec(memory_space=pl.ANY)],
        out_specs=(pl.BlockSpec(memory_space=pl.ANY), pl.BlockSpec(memory_space=pltpu.VMEM)),
        scratch_shapes=[
            vmem(1024, 1024),
            vmem(1024, B), vmem(B, 1024),
            vmem(2, 1024, B), vmem(2, B, 1024),
            vmem(2, 1024, B), vmem(2, B, 1024),
            vmem(B, 1024),
            vmem(2, 1024, B), vmem(2, B, 1024),
            vmem(2, 512, B), vmem(2, 8, 64, B), vmem(2, 16, 16, 1024),
            vmem(2, 1024, B), vmem(2, B, 1024),
            vmem(2, 2, 16, 16, B), vmem(2, 16, 32, B), vmem(2, 16, 48, B),
            vmem(B, 2 * B),
            vmem(1024, 2 * B), vmem(2 * B, 1024),
            vmem(2, B, B),
            pltpu.SemaphoreType.DMA((4,)),
            pltpu.SemaphoreType.DMA((480,)),
            pltpu.SemaphoreType.DMA((480,)),
        ],
        compiler_params=pltpu.CompilerParams(
            collective_id=0, has_side_effects=True, vmem_limit_bytes=60 * 1024 * 1024
        ),
    )(matrix_cyclic)


def solution(mesh):
    return jax.shard_map(
        shards,
        mesh=mesh,
        in_specs=(P("row", "col"),),
        out_specs=(P("row", "col"), P()),
        check_vma=False,
    )
```

```python
import functools
import math

import jax
import jax.numpy as jnp
from jax import lax
from jax.experimental import pallas as pl
from jax.experimental.pallas import tpu as pltpu
from jax.sharding import PartitionSpec as P

B = 256
F32 = jnp.float32
HIGH = lax.Precision.HIGH
HIGHEST = lax.Precision.HIGHEST
NN = (((1,), (0,)), ((), ()))
NT = (((1,), (1,)), ((), ()))
TN = (((0,), (0,)), ((), ()))


def dot(left, right, dims=NN, precision=HIGH):
    return lax.dot_general(left, right, dims, precision=precision, preferred_element_type=F32)


class Place:
    def __init__(self):
        self.row = lax.axis_index("row")
        self.col = lax.axis_index("col")
        self.x, self.y = self.row // 4, lax.rem(self.row, 4)
        self.z, self.core = self.col // 2, lax.rem(self.col, 2)
        self.slot = self.core * 8 + self.z

    def z_peer(self, d):
        return (self.row, lax.rem(self.z + d, 8) * 2 + self.core)

    def z_slot_to(self, d):
        return self.core * 8 + lax.rem(self.z + d, 8)

    def z_slot_from(self, d):
        return self.core * 8 + lax.rem(self.z + 8 - d, 8)

    def sibling(self):
        return (self.row, self.col + 1 - 2 * self.core)

    def col_peer(self, t):
        return (self.row, lax.rem(self.col + t, 16))

    def col_slot_to(self, t):
        other = lax.rem(self.col + t, 16)
        return lax.rem(other, 2) * 8 + other // 2

    def row_peer(self, d):
        return (self.row_to(d), self.col)

    def row_to(self, d):
        return lax.rem(self.x + d // 4, 4) * 4 + lax.rem(self.y + lax.rem(d, 4), 4)

    def row_from(self, d):
        return lax.rem(self.x + 4 - d // 4, 4) * 4 + lax.rem(self.y + 4 - lax.rem(d, 4), 4)


def loop(start, stop, body):
    def step(i, carry):
        body(i)
        return carry

    lax.fori_loop(start, stop, step, 0)


class Comm:
    def __init__(self, place, send, recv):
        self.at = place
        self.send = send
        self.recv = recv
        self.used = 0
        self.sent = []

    def take(self, count):
        base = self.used
        self.used += count
        return base

    def copy(self, src, dst, send_index, recv_index, device):
        return pltpu.make_async_remote_copy(
            src_ref=src,
            dst_ref=dst,
            send_sem=self.send.at[send_index],
            recv_sem=self.recv.at[recv_index],
            device_id=device,
            device_id_type=pl.DeviceIdType.MESH,
        )

    def finish(self):
        for wait in self.sent:
            wait()


class Exchange:
    def __init__(self, comm, first, stop, peer, src, dst, landed):
        self.comm, self.first, self.stop = comm, first, stop
        self.peer, self.src, self.dst, self.landed = peer, src, dst, landed
        self.base = comm.take(stop - first) - first
        comm.sent.append(self.wait_sends)

    def start_one(self, d):
        i = self.base + d
        self.comm.copy(self.src(d), self.dst(d), i, i, self.peer(d)).start()

    def start(self):
        loop(self.first, self.stop, self.start_one)

    def wait_one(self, d):
        i = self.base + d
        self.comm.copy(self.landed(d), self.landed(d), i, i, self.peer(d)).wait_recv()

    def wait(self):
        loop(self.first, self.stop, self.wait_one)

    def wait_sends(self):
        def one(d):
            i = self.base + d
            self.comm.copy(self.src(d), self.dst(d), i, i, self.peer(d)).wait_send()

        loop(self.first, self.stop, one)


class Deal:
    def __init__(self, comm, source, peer, src, dst, landed):
        self.comm, self.source = comm, source
        self.peer, self.src, self.dst, self.landed = peer, src, dst, landed
        self.base = comm.take(16)
        comm.sent.append(self.wait_sends)

    def copy(self, t):
        return self.comm.copy(self.src(t), self.dst(t), self.base + t, self.base, self.peer(t))

    def start(self):
        @pl.when(self.source)
        def _():
            loop(1, 16, lambda t: self.copy(t).start())

    def wait(self):
        @pl.when(jnp.logical_not(self.source))
        def _():
            self.comm.copy(self.landed, self.landed, self.base, self.base, self.peer(1)).wait_recv()

    def wait_sends(self):
        @pl.when(self.source)
        def _():
            loop(1, 16, lambda t: self.copy(t).wait_send())


class GatherCol:
    def __init__(self, comm, part):
        at = comm.at
        self.at = at
        self.z = Exchange(
            comm, 1, 8, at.z_peer, lambda d: part(at.slot), lambda d: part(at.slot), lambda d: part(at.z_slot_from(d))
        )
        sibling = lambda d: at.sibling()
        other = lambda d: (1 - at.core) * 8 + lax.rem(at.z + 8 - d, 8)
        self.pair = Exchange(
            comm, 0, 8, sibling, lambda d: part(at.z_slot_from(d)), lambda d: part(at.z_slot_from(d)),
            lambda d: part(other(d)),
        )

    def start(self):
        self.z.start()
        self.pair.start_one(0)

    def forward(self):
        def one(d):
            self.z.wait_one(d)
            self.pair.start_one(d)

        loop(1, 8, one)

    def wait(self):
        self.pair.wait()


def cholesky_block(aug, block):
    sub = lax.broadcasted_iota(jnp.int32, (8, 128), 0)
    lane = lax.broadcasted_iota(jnp.int32, (8, 128), 1)
    base = 64 * block
    first = 128 * (base // 128)
    offset = base - first

    def strip(i):
        rows = pl.ds(pl.multiple_of(base + 8 * i, 8), 8)
        diag = pltpu.roll(aug[rows, first : first + 128], lax.rem(128 - offset - 8 * i, 128), 1)
        parts = [aug[rows, 128 * k : 128 * k + 128] for k in range(4)]
        cols = [jnp.broadcast_to(diag[:, j : j + 1], (8, 128)) for j in range(8)]
        pivots = jnp.ones((8, 128), F32)
        for j in range(8):
            pivot = jnp.broadcast_to(cols[j][j : j + 1, :], (8, 128))
            pivots = jnp.where(sub == j, pivot, pivots)
            scale = jnp.where(sub > j, cols[j] * (1.0 / pivot), 0.0)
            for k in range(j + 1, 8):
                cols[k] = cols[k] - scale * jnp.broadcast_to(cols[k][j : j + 1, :], (8, 128))
            for k in range(4):
                parts[k] = parts[k] - scale * jnp.broadcast_to(parts[k][j : j + 1, :], (8, 128))
        norm = 1.0 / jnp.sqrt(pivots)
        parts = [part * norm for part in parts]
        factors = jnp.where(lane >= offset + 8 * (i + 1), parts[first // 128], 0.0).T
        for t in range(8):
            below = slice(base + 8 * t, base + 8 * t + 8)
            spread = [
                jnp.broadcast_to(factors[offset + 8 * t : offset + 8 * t + 8, j : j + 1], (8, 128)) for j in range(8)
            ]
            for k in range(4):
                lanes = slice(128 * k, 128 * k + 128)
                rest = aug[below, lanes]
                for j in range(8):
                    rest = rest - spread[j] * jnp.broadcast_to(parts[k][j : j + 1, :], (8, 128))
                aug[below, lanes] = rest
        for k in range(4):
            aug[rows, 128 * k : 128 * k + 128] = parts[k]

    loop(0, 8, strip)
    if base + 64 < B:
        done = aug[base : base + 64, :]
        aug[base + 64 :, :] = aug[base + 64 :, :] - dot(done[:, base + 64 : B], done, TN, HIGHEST)


def kernel(a_ref, out_ref, band_ref, g, stage_r, stage_c, pr, pc, er, ec, prt, ypr, ypc, half, zr, xr, yr, yc,
           gx, sm1, sm2, top1, top2, aug, left, right, small, local_sem, send_sem, recv_sem):
    at = Place()
    comm = Comm(at, send_sem, recv_sem)
    row, col, slot = at.row, at.col, at.slot
    load = pltpu.make_async_copy(a_ref, g, local_sem.at[0])
    load.start()
    barrier = pltpu.get_barrier_semaphore()

    def greet(t):
        pl.semaphore_signal(barrier, inc=1, device_id=at.col_peer(t), device_id_type=pl.DeviceIdType.MESH)
        pl.semaphore_signal(barrier, inc=1, device_id=at.row_peer(t), device_id_type=pl.DeviceIdType.MESH)

    loop(1, 16, greet)
    load.wait()
    pl.semaphore_wait(barrier, 30)

    def rows64(ref, s):
        return ref.at[pl.ds(pl.multiple_of(64 * s, 64), 64)]

    def rows16(ref, s):
        return ref.at[pl.ds(pl.multiple_of(16 * s, 16), 16)]

    class Spread:
        def __init__(self, b, to_r, to_c):
            self.b, self.to_r, self.to_c = b, to_r, to_c
            self.deal_r = Deal(
                comm, col == b, at.col_peer,
                lambda t: rows64(stage_r, at.col_slot_to(t)), lambda t: rows64(to_r, at.col_slot_to(t)),
                rows64(to_r, slot),
            )
            self.deal_c = Deal(
                comm, row == b, at.row_peer,
                lambda t: rows16(stage_c, at.row_to(t)), lambda t: rows16(to_c, at.row_to(t)), rows16(to_c, row),
            )
            self.gather_r = GatherCol(comm, lambda s: rows64(to_r, s))
            self.gather_c = Exchange(
                comm, 1, 16, at.row_peer, lambda d: rows16(to_c, row), lambda d: rows16(to_c, row),
                lambda d: rows16(to_c, at.row_from(d)),
            )

        def deal(self, masked):
            @pl.when(col == self.b)
            def _():
                stage_r[...] = g[:, 0:B]
                if masked:
                    @pl.when(row == 0)
                    def _():
                        stage_r[0:B, :] = jnp.zeros((B, B), F32)
                mine = pl.ds(pl.multiple_of(64 * slot, 64), 64)
                self.to_r[mine, :] = stage_r[mine, :]

            self.deal_r.start()

            @pl.when(row == self.b)
            def _():
                stage_c[...] = g[0:B, :]
                if masked:
                    @pl.when(col == 0)
                    def _():
                        stage_c[:, 0:B] = jnp.zeros((B, B), F32)
                mine = pl.ds(pl.multiple_of(16 * row, 16), 16)
                self.to_c[mine, :] = stage_c[mine, :]

            self.deal_c.start()

        def gather(self):
            self.deal_r.wait()
            self.gather_r.start()
            self.deal_c.wait()
            self.gather_c.start()

        def forward(self):
            self.gather_r.forward()

        def wait(self):
            self.gather_r.wait()
            self.gather_c.wait()

    def panel(p, spread_e, tops1):
        panel_r, panel_c, side_r, side_c = pr.at[p], pc.at[p], er.at[p], ec.at[p]
        top = p + 1
        full_r, full_c = yr.at[p], yc.at[p]
        mine16 = pl.ds(pl.multiple_of(16 * slot, 16), 16)
        own16 = pl.ds(pl.multiple_of(16 * row, 16), 16)
        mine64 = pl.ds(pl.multiple_of(64 * slot, 64), 64)
        mine8 = pl.ds(pl.multiple_of(8 * at.core, 8), 8)

        def row_sum(which, sums):
            got = gx.at[p, which]
            ring = Exchange(comm, 1, 16, at.row_peer, lambda d: got.at[0], lambda d: got.at[d], lambda d: got.at[d])
            gather = GatherCol(comm, lambda s: sums.at[s])

            def begin(value):
                got[0] = value
                ring.start()

            def reduce():
                ring.wait()
                total = got[0]
                for d in range(1, 16):
                    total = total + got[d]
                sums[slot] = total
                gather.start()

            def end():
                gather.forward()
                gather.wait()

            return begin, reduce, end

        gram_begin, gram_reduce, gram_end = row_sum(0, sm1.at[p])
        inner_begin, inner_reduce, inner_end = row_sum(1, sm2.at[p])
        tops2 = Tops(top, top2.at[p])

        prt[...] = panel_r[...].T
        gram_begin(dot(prt[mine16, :], panel_r[...], NN, HIGHEST))

        if p == 1:
            @pl.when(col == top)
            def _():
                top1[p, row] = panel_c[own16, 0:B]

            tops1.deal.start()

            def update(n):
                lanes = pl.ds(pl.multiple_of(n * B, B), B)
                g[:, lanes] = g[:, lanes] - dot(left[...], right[:, lanes])

            loop(0, 4, update)
            spread_e.deal(False)

        pair = Exchange(
            comm, 0, 1, lambda d: at.sibling(),
            lambda d: ypr.at[p, pl.ds(pl.multiple_of(8 * (1 - at.core), 8), 8)], lambda d: half.at[p],
            lambda d: half.at[p],
        )
        cross = Exchange(
            comm, 1, 8, at.z_peer, lambda d: ypr.at[p, at.z_slot_to(d)], lambda d: zr.at[p, d], lambda d: zr.at[p, d]
        )
        ring = Exchange(
            comm, 1, 16, at.row_peer, lambda d: rows16(ypc.at[p], at.row_to(d)), lambda d: xr.at[p, d],
            lambda d: xr.at[p, d],
        )

        def product_rows(m):
            rows = pl.ds(pl.multiple_of(m * B, B), B)
            value = dot(g[rows, :], panel_c[...], NT)
            ypr[p, pl.ds(pl.multiple_of(4 * m, 4), 4), 0:64, :] = value.reshape(4, 64, B)

        def product_cols(n):
            lanes = pl.ds(pl.multiple_of(n * B, B), B)
            ypc[p, :, lanes] = dot(prt[...], g[:, lanes])

        loop(0, 4, product_rows)
        ypr[p, :, 64:80, :] = dot(prt[...], ypr[p, :, 0:64, :].reshape(4 * B, B)).reshape(16, 16, B)
        pair.start()
        loop(0, 2, product_cols)
        gram_reduce()
        pair.wait()
        ypr[p, mine8] = ypr[p, mine8] + half[p]
        cross.start()
        loop(2, 4, product_cols)
        ring.start()
        if p == 0:
            spread_e.forward()
        else:
            tops1.gather()
            spread_e.gather()

        gram_end()
        eye = (lax.broadcasted_iota(jnp.int32, (B, B), 0) == lax.broadcasted_iota(jnp.int32, (B, B), 1)).astype(F32)
        aug[:, 0:B] = sm1[p].reshape(B, B)
        aug[:, B : 2 * B] = eye
        cholesky_block(aug, 0)

        gather_r = GatherCol(comm, lambda s: rows64(full_r, s))
        gather_c = Exchange(
            comm, 1, 16, at.row_peer, lambda d: rows16(full_c, row), lambda d: rows16(full_c, row),
            lambda d: rows16(full_c, at.row_from(d)),
        )
        cross.wait()
        total = ypr[p, slot]
        for d in range(1, 8):
            total = total + zr[p, d]
        inner_begin(total[64:80, :])
        full_r[mine64, :] = total[0:64, :]
        gather_r.start()
        ring.wait()
        total = ypc[p, own16, :]
        for d in range(1, 16):
            total = total + xr[p, d]
        full_c[own16, :] = total

        @pl.when(col == top)
        def _():
            top2[p, row, 0:16, :] = total[:, 0:B]
            top2[p, row, 16:32, :] = side_c[own16, 0:B]

        tops2.deal.start()
        gather_c.start()
        cholesky_block(aug, 1)
        inner_reduce()
        tops2.gather()
        cholesky_block(aug, 2)
        cholesky_block(aug, 3)

        upper = jnp.where(
            lax.broadcasted_iota(jnp.int32, (B, B), 1) >= lax.broadcasted_iota(jnp.int32, (B, B), 0), aug[:, 0:B], 0.0
        )
        band_ref[p] = upper / 128.0
        inverse = aug[:, B : 2 * B]
        tops1.ring.wait()
        c_t = dot(inverse, top1[p].reshape(B, B))
        power = c_t
        inverse_t = eye + power
        for _ in range(5):
            power = dot(power, power)
            inverse_t = inverse_t + dot(inverse_t, power)
        small[2] = inverse_t
        small[3] = dot(inverse, inverse_t, TN)

        def w_rows(m):
            rows = pl.ds(pl.multiple_of(m * B, B), B)
            left[rows, 0:B] = -dot(panel_r[rows, :], aug[:, B : 2 * B], NT)

        def w_cols(n):
            lanes = pl.ds(pl.multiple_of(n * B, B), B)
            right[B : 2 * B, lanes] = -dot(aug[:, B : 2 * B], panel_c[:, lanes])

        loop(0, 4, w_rows)
        loop(0, 4, w_cols)

        @pl.when(row == top)
        def _():
            left[0:B, 0:B] = left[0:B, 0:B] + eye

        @pl.when(col == top)
        def _():
            right[B : 2 * B, 0:B] = right[B : 2 * B, 0:B] + eye

        if p == 1:
            spread_e.forward()
        gather_r.forward()
        spread_e.wait()
        gather_r.wait()

        def u_rows(m):
            rows = pl.ds(pl.multiple_of(m * B, B), B)
            left[rows, B : 2 * B] = dot(side_r[rows, :], small[2]) - dot(full_r[rows, :], small[3])

        def u_cols(n):
            lanes = pl.ds(pl.multiple_of(n * B, B), B)
            right[0:B, lanes] = dot(small[2], side_c[:, lanes], TN) - dot(small[3], full_c[:, lanes], TN)

        loop(0, 4, u_rows)
        gather_c.wait()
        loop(0, 4, u_cols)

        inner_end()
        tops2.ring.wait()
        y_top = top2[p, :, 0:16, :].reshape(B, B)
        e_top = top2[p, :, 16:32, :].reshape(B, B)
        y_top = dot(inverse, y_top)
        x_top = e_top - y_top.T
        middle = x_top - y_top + dot(dot(inverse, sm2[p].reshape(B, B)), inverse, NT)
        half_sym = 0.5 * dot(inverse_t, dot(middle, inverse_t), TN)
        small[4] = half_sym

        def end_rows(m):
            rows = pl.ds(pl.multiple_of(m * B, B), B)
            left[rows, B : 2 * B] = left[rows, B : 2 * B] - dot(left[rows, 0:B], small[4])

        def end_cols(n):
            lanes = pl.ds(pl.multiple_of(n * B, B), B)
            right[0:B, lanes] = right[0:B, lanes] - dot(small[4], right[B : 2 * B, lanes], TN)

        loop(0, 4, end_rows)
        loop(0, 4, end_cols)
        if p == 1:
            return
        w_top_t = eye - c_t
        small[0] = w_top_t
        small[1] = dot(x_top, inverse_t) - dot(w_top_t, half_sym, TN)

        def next_rows(m):
            rows = pl.ds(pl.multiple_of(m * B, B), B)
            pr[1, rows, :] = (
                side_r[rows, :] - dot(left[rows, 0:B], small[1], NT) - dot(left[rows, B : 2 * B], small[0])
            )

        loop(0, 4, next_rows)

        @pl.when(row < 2)
        def _():
            pr[1, 0:B, :] = jnp.zeros((B, B), F32)

        def next_cols(n):
            lanes = pl.ds(pl.multiple_of(n * B, B), B)
            pc[1, :, lanes] = (
                side_c[:, lanes] - dot(small[1], right[B : 2 * B, lanes]) - dot(small[0], right[0:B, lanes], TN)
            )

        loop(0, 4, next_cols)

        @pl.when(col < 2)
        def _():
            pc[1, :, 0:B] = jnp.zeros((B, B), F32)

    class Tops:
        def __init__(self, source, slabs):
            own = slabs.at[row]
            self.deal = Deal(comm, col == source, at.col_peer, lambda t: own, lambda t: own, own)
            self.ring = Exchange(
                comm, 1, 16, at.row_peer, lambda d: own, lambda d: own, lambda d: slabs.at[at.row_from(d)]
            )

        def gather(self):
            self.deal.wait()
            self.ring.start()

    spread_p = Spread(0, pr.at[0], pc.at[0])
    spread_e = Spread(1, er.at[0], ec.at[0])
    tops_first = Tops(1, top1.at[0])
    spread_p.deal(True)
    spread_e.deal(False)
    spread_p.gather()

    @pl.when(col == 1)
    def _():
        top1[0, row] = pc[0, pl.ds(pl.multiple_of(16 * row, 16), 16), 0:B]

    tops_first.deal.start()
    spread_e.gather()
    tops_first.gather()
    spread_p.forward()
    spread_p.wait()
    panel(0, spread_e, tops_first)
    panel(1, Spread(2, er.at[1], ec.at[1]), Tops(2, top1.at[1]))

    def last(n):
        lanes = pl.ds(pl.multiple_of(n * B, B), B)
        g[:, lanes] = g[:, lanes] - dot(left[...], right[:, lanes])

        @pl.when(row < 2)
        def _():
            g[0:B, lanes] = jnp.zeros((B, B), F32)

        @pl.when(jnp.logical_and(col < 2, n == 0))
        def _():
            g[:, lanes] = jnp.zeros((4 * B, B), F32)

        pltpu.make_async_copy(g.at[:, lanes], out_ref.at[:, lanes], local_sem.at[n]).start()

    loop(0, 4, last)
    comm.finish()

    def drain(n):
        lanes = pl.ds(pl.multiple_of(n * B, B), B)
        pltpu.make_async_copy(g.at[:, lanes], out_ref.at[:, lanes], local_sem.at[n]).wait()

    loop(0, 4, drain)


def shards(matrix_cyclic):
    vmem = lambda *shape: pltpu.VMEM(shape, F32)
    return pl.pallas_call(
        kernel,
        out_shape=(
            jax.ShapeDtypeStruct((1024, 1024), F32),
            jax.ShapeDtypeStruct((2, B, B), F32),
        ),
        in_specs=[pl.BlockSpec(memory_space=pl.ANY)],
        out_specs=(pl.BlockSpec(memory_space=pl.ANY), pl.BlockSpec(memory_space=pltpu.VMEM)),
        scratch_shapes=[
            vmem(1024, 1024),
            vmem(1024, B), vmem(B, 1024),
            vmem(2, 1024, B), vmem(2, B, 1024),
            vmem(2, 1024, B), vmem(2, B, 1024),
            vmem(B, 1024),
            vmem(2, 16, 80, B), vmem(2, B, 1024),
            vmem(2, 8, 80, B), vmem(2, 8, 80, B), vmem(2, 16, 16, 1024),
            vmem(2, 1024, B), vmem(2, B, 1024),
            vmem(2, 2, 16, 16, B), vmem(2, 16, 16, B), vmem(2, 16, 16, B),
            vmem(2, 16, 16, B), vmem(2, 16, 32, B),
            vmem(B, 2 * B),
            vmem(1024, 2 * B), vmem(2 * B, 1024),
            vmem(5, B, B),
            pltpu.SemaphoreType.DMA((4,)),
            pltpu.SemaphoreType.DMA((544,)),
            pltpu.SemaphoreType.DMA((544,)),
        ],
        compiler_params=pltpu.CompilerParams(
            collective_id=0, has_side_effects=True, vmem_limit_bytes=60 * 1024 * 1024
        ),
    )(matrix_cyclic)


def solution(mesh):
    return jax.shard_map(
        shards,
        mesh=mesh,
        in_specs=(P("row", "col"),),
        out_specs=(P("row", "col"), P()),
        check_vma=False,
    )
```

```python
import functools
import math

import jax
import jax.numpy as jnp
from jax import lax
from jax.experimental import pallas as pl
from jax.experimental.pallas import tpu as pltpu
from jax.sharding import PartitionSpec as P

B = 256
F32 = jnp.float32
HIGH = lax.Precision.HIGH
HIGHEST = lax.Precision.HIGHEST
NN = (((1,), (0,)), ((), ()))
NT = (((1,), (1,)), ((), ()))
TN = (((0,), (0,)), ((), ()))


def dot(left, right, dims=NN, precision=HIGH):
    return lax.dot_general(left, right, dims, precision=precision, preferred_element_type=F32)


class Place:
    def __init__(self):
        self.row = lax.axis_index("row")
        self.col = lax.axis_index("col")
        self.x, self.y = self.row // 4, lax.rem(self.row, 4)
        self.z, self.core = self.col // 2, lax.rem(self.col, 2)
        self.slot = self.core * 8 + self.z

    def z_peer(self, d):
        return (self.row, lax.rem(self.z + d, 8) * 2 + self.core)

    def z_slot_to(self, d):
        return self.core * 8 + lax.rem(self.z + d, 8)

    def z_slot_from(self, d):
        return self.core * 8 + lax.rem(self.z + 8 - d, 8)

    def sibling(self):
        return (self.row, self.col + 1 - 2 * self.core)

    def col_peer(self, t):
        return (self.row, lax.rem(self.col + t, 16))

    def col_slot_to(self, t):
        other = lax.rem(self.col + t, 16)
        return lax.rem(other, 2) * 8 + other // 2

    def row_peer(self, d):
        return (self.row_to(d), self.col)

    def row_to(self, d):
        return lax.rem(self.x + d // 4, 4) * 4 + lax.rem(self.y + lax.rem(d, 4), 4)

    def row_from(self, d):
        return lax.rem(self.x + 4 - d // 4, 4) * 4 + lax.rem(self.y + 4 - lax.rem(d, 4), 4)


def loop(start, stop, body):
    def step(i, carry):
        body(i)
        return carry

    lax.fori_loop(start, stop, step, 0)


class Comm:
    def __init__(self, place, send, recv):
        self.at = place
        self.send = send
        self.recv = recv
        self.used = 0
        self.sent = []

    def take(self, count):
        base = self.used
        self.used += count
        return base

    def copy(self, src, dst, send_index, recv_index, device):
        return pltpu.make_async_remote_copy(
            src_ref=src,
            dst_ref=dst,
            send_sem=self.send.at[send_index],
            recv_sem=self.recv.at[recv_index],
            device_id=device,
            device_id_type=pl.DeviceIdType.MESH,
        )

    def finish(self):
        for wait in self.sent:
            wait()
        self.sent = []


class Exchange:
    def __init__(self, comm, first, stop, peer, src, dst, landed):
        self.comm, self.first, self.stop = comm, first, stop
        self.peer, self.src, self.dst, self.landed = peer, src, dst, landed
        self.base = comm.take(stop - first) - first
        comm.sent.append(self.wait_sends)

    def start_one(self, d):
        i = self.base + d
        self.comm.copy(self.src(d), self.dst(d), i, i, self.peer(d)).start()

    def start(self):
        loop(self.first, self.stop, self.start_one)

    def wait_one(self, d):
        i = self.base + d
        self.comm.copy(self.landed(d), self.landed(d), i, i, self.peer(d)).wait_recv()

    def wait(self):
        loop(self.first, self.stop, self.wait_one)

    def wait_sends(self):
        def one(d):
            i = self.base + d
            self.comm.copy(self.src(d), self.dst(d), i, i, self.peer(d)).wait_send()

        loop(self.first, self.stop, one)


class Deal:
    def __init__(self, comm, source, peer, src, dst, landed):
        self.comm, self.source = comm, source
        self.peer, self.src, self.dst, self.landed = peer, src, dst, landed
        self.base = comm.take(16)
        comm.sent.append(self.wait_sends)

    def copy(self, t):
        return self.comm.copy(self.src(t), self.dst(t), self.base + t, self.base, self.peer(t))

    def start(self):
        @pl.when(self.source)
        def _():
            loop(1, 16, lambda t: self.copy(t).start())

    def wait(self):
        @pl.when(jnp.logical_not(self.source))
        def _():
            self.comm.copy(self.landed, self.landed, self.base, self.base, self.peer(1)).wait_recv()

    def wait_sends(self):
        @pl.when(self.source)
        def _():
            loop(1, 16, lambda t: self.copy(t).wait_send())


class GatherCol:
    def __init__(self, comm, part):
        at = comm.at
        self.at = at
        self.z = Exchange(
            comm, 1, 8, at.z_peer, lambda d: part(at.slot), lambda d: part(at.slot), lambda d: part(at.z_slot_from(d))
        )
        sibling = lambda d: at.sibling()
        other = lambda d: (1 - at.core) * 8 + lax.rem(at.z + 8 - d, 8)
        self.pair = Exchange(
            comm, 0, 8, sibling, lambda d: part(at.z_slot_from(d)), lambda d: part(at.z_slot_from(d)),
            lambda d: part(other(d)),
        )

    def start(self):
        self.z.start()
        self.pair.start_one(0)

    def forward(self):
        def one(d):
            self.z.wait_one(d)
            self.pair.start_one(d)

        loop(1, 8, one)

    def wait(self):
        self.pair.wait()


def cholesky_block(aug, block):
    sub = lax.broadcasted_iota(jnp.int32, (8, 128), 0)
    lane = lax.broadcasted_iota(jnp.int32, (8, 128), 1)
    base = 64 * block
    first = 128 * (base // 128)
    offset = base - first

    def strip(i):
        rows = pl.ds(pl.multiple_of(base + 8 * i, 8), 8)
        diag = pltpu.roll(aug[rows, first : first + 128], lax.rem(128 - offset - 8 * i, 128), 1)
        parts = [aug[rows, 128 * k : 128 * k + 128] for k in range(4)]
        cols = [jnp.broadcast_to(diag[:, j : j + 1], (8, 128)) for j in range(8)]
        pivots = jnp.ones((8, 128), F32)
        for j in range(8):
            pivot = jnp.broadcast_to(cols[j][j : j + 1, :], (8, 128))
            pivots = jnp.where(sub == j, pivot, pivots)
            scale = jnp.where(sub > j, cols[j] * (1.0 / pivot), 0.0)
            for k in range(j + 1, 8):
                cols[k] = cols[k] - scale * jnp.broadcast_to(cols[k][j : j + 1, :], (8, 128))
            for k in range(4):
                parts[k] = parts[k] - scale * jnp.broadcast_to(parts[k][j : j + 1, :], (8, 128))
        norm = 1.0 / jnp.sqrt(pivots)
        parts = [part * norm for part in parts]
        factors = jnp.where(lane >= offset + 8 * (i + 1), parts[first // 128], 0.0).T
        for t in range(8):
            below = slice(base + 8 * t, base + 8 * t + 8)
            spread = [
                jnp.broadcast_to(factors[offset + 8 * t : offset + 8 * t + 8, j : j + 1], (8, 128)) for j in range(8)
            ]
            for k in range(4):
                lanes = slice(128 * k, 128 * k + 128)
                rest = aug[below, lanes]
                for j in range(8):
                    rest = rest - spread[j] * jnp.broadcast_to(parts[k][j : j + 1, :], (8, 128))
                aug[below, lanes] = rest
        for k in range(4):
            aug[rows, 128 * k : 128 * k + 128] = parts[k]

    loop(0, 8, strip)
    if base + 64 < B:
        done = aug[base : base + 64, :]
        aug[base + 64 :, :] = aug[base + 64 :, :] - dot(done[:, base + 64 : B], done, TN, HIGHEST)


def kernel(a_ref, out_ref, band_ref, g, stage_r, stage_c, pr, pc, er, ec, prt, ypr, ypc, half, zr, xr, yr, yc,
           gx, sm1, sm2, top1, top2, aug, left, right, small, local_sem, send_sem, recv_sem):
    at = Place()
    comm = Comm(at, send_sem, recv_sem)
    row, col, slot = at.row, at.col, at.slot
    load = pltpu.make_async_copy(a_ref, g, local_sem.at[0])
    load.start()
    barrier = pltpu.get_barrier_semaphore()

    def greet(t):
        pl.semaphore_signal(barrier, inc=1, device_id=at.col_peer(t), device_id_type=pl.DeviceIdType.MESH)
        pl.semaphore_signal(barrier, inc=1, device_id=at.row_peer(t), device_id_type=pl.DeviceIdType.MESH)

    loop(1, 16, greet)
    load.wait()
    pl.semaphore_wait(barrier, 30)

    def rows64(ref, s):
        return ref.at[pl.ds(pl.multiple_of(64 * s, 64), 64)]

    def rows16(ref, s):
        return ref.at[pl.ds(pl.multiple_of(16 * s, 16), 16)]

    class Spread:
        def __init__(self, b, to_r, to_c):
            self.b, self.to_r, self.to_c = b, to_r, to_c
            self.deal_r = Deal(
                comm, col == b, at.col_peer,
                lambda t: rows64(stage_r, at.col_slot_to(t)), lambda t: rows64(to_r, at.col_slot_to(t)),
                rows64(to_r, slot),
            )
            self.deal_c = Deal(
                comm, row == b, at.row_peer,
                lambda t: rows16(stage_c, at.row_to(t)), lambda t: rows16(to_c, at.row_to(t)), rows16(to_c, row),
            )
            self.gather_r = GatherCol(comm, lambda s: rows64(to_r, s))
            self.gather_c = Exchange(
                comm, 1, 16, at.row_peer, lambda d: rows16(to_c, row), lambda d: rows16(to_c, row),
                lambda d: rows16(to_c, at.row_from(d)),
            )

        def deal(self, masked):
            @pl.when(col == self.b)
            def _():
                stage_r[...] = g[:, 0:B]
                if masked:
                    @pl.when(row == 0)
                    def _():
                        stage_r[0:B, :] = jnp.zeros((B, B), F32)
                mine = pl.ds(pl.multiple_of(64 * slot, 64), 64)
                self.to_r[mine, :] = stage_r[mine, :]

            self.deal_r.start()

            @pl.when(row == self.b)
            def _():
                stage_c[...] = g[0:B, :]
                if masked:
                    @pl.when(col == 0)
                    def _():
                        stage_c[:, 0:B] = jnp.zeros((B, B), F32)
                mine = pl.ds(pl.multiple_of(16 * row, 16), 16)
                self.to_c[mine, :] = stage_c[mine, :]

            self.deal_c.start()

        def gather(self):
            self.deal_r.wait()
            self.gather_r.start()
            self.deal_c.wait()
            self.gather_c.start()

        def forward(self):
            self.gather_r.forward()

        def wait(self):
            self.gather_r.wait()
            self.gather_c.wait()

    def panel(p, spread_e, tops1):
        panel_r, panel_c, side_r, side_c = pr.at[p], pc.at[p], er.at[p], ec.at[p]
        top = p + 1
        full_r, full_c = yr.at[p], yc.at[p]
        mine16 = pl.ds(pl.multiple_of(16 * slot, 16), 16)
        own16 = pl.ds(pl.multiple_of(16 * row, 16), 16)
        mine64 = pl.ds(pl.multiple_of(64 * slot, 64), 64)
        mine8 = pl.ds(pl.multiple_of(8 * at.core, 8), 8)

        def row_sum(which, sums):
            got = gx.at[p, which]
            ring = Exchange(comm, 1, 16, at.row_peer, lambda d: got.at[0], lambda d: got.at[d], lambda d: got.at[d])
            gather = GatherCol(comm, lambda s: sums.at[s])

            def begin(value):
                got[0] = value
                ring.start()

            def reduce():
                ring.wait()
                total = got[0]
                for d in range(1, 16):
                    total = total + got[d]
                sums[slot] = total
                gather.start()

            def end():
                gather.forward()
                gather.wait()

            return begin, reduce, end

        gram_begin, gram_reduce, gram_end = row_sum(0, sm1.at[p])
        inner_begin, inner_reduce, inner_end = row_sum(1, sm2.at[p])
        tops2 = Tops(top, top2.at[p])

        prt[...] = panel_r[...].T
        gram_begin(dot(prt[mine16, :], panel_r[...], NN, HIGHEST))

        if p == 1:
            @pl.when(col == top)
            def _():
                top1[p, row] = panel_c[own16, 0:B]

            tops1.deal.start()

            def update(n):
                lanes = pl.ds(pl.multiple_of(n * B, B), B)
                g[:, lanes] = g[:, lanes] - dot(left[...], right[:, lanes])

            loop(0, 4, update)
            spread_e.deal(False)

        pair = Exchange(
            comm, 0, 1, lambda d: at.sibling(),
            lambda d: ypr.at[p, pl.ds(pl.multiple_of(8 * (1 - at.core), 8), 8)], lambda d: half.at[p],
            lambda d: half.at[p],
        )
        cross = Exchange(
            comm, 1, 8, at.z_peer, lambda d: ypr.at[p, at.z_slot_to(d)], lambda d: zr.at[p, d], lambda d: zr.at[p, d]
        )
        ring = Exchange(
            comm, 1, 16, at.row_peer, lambda d: rows16(ypc.at[p], at.row_to(d)), lambda d: xr.at[p, d],
            lambda d: xr.at[p, d],
        )

        def product_rows(m):
            rows = pl.ds(pl.multiple_of(m * B, B), B)
            value = dot(g[rows, :], panel_c[...], NT)
            ypr[p, pl.ds(pl.multiple_of(4 * m, 4), 4), 0:64, :] = value.reshape(4, 64, B)

        def product_cols(n):
            lanes = pl.ds(pl.multiple_of(n * B, B), B)
            ypc[p, :, lanes] = dot(prt[...], g[:, lanes])

        loop(0, 4, product_rows)
        ypr[p, :, 64:80, :] = dot(prt[...], ypr[p, :, 0:64, :].reshape(4 * B, B)).reshape(16, 16, B)
        pair.start()
        loop(0, 2, product_cols)
        gram_reduce()
        pair.wait()
        ypr[p, mine8] = ypr[p, mine8] + half[p]
        cross.start()
        loop(2, 4, product_cols)
        ring.start()
        if p == 1:
            tops1.gather()
            spread_e.gather()

        gram_end()
        eye = (lax.broadcasted_iota(jnp.int32, (B, B), 0) == lax.broadcasted_iota(jnp.int32, (B, B), 1)).astype(F32)
        aug[:, 0:B] = sm1[p].reshape(B, B)
        aug[:, B : 2 * B] = eye
        cholesky_block(aug, 0)

        gather_r = GatherCol(comm, lambda s: rows64(full_r, s))
        gather_c = Exchange(
            comm, 1, 16, at.row_peer, lambda d: rows16(full_c, row), lambda d: rows16(full_c, row),
            lambda d: rows16(full_c, at.row_from(d)),
        )
        cross.wait()
        total = ypr[p, slot]
        for d in range(1, 8):
            total = total + zr[p, d]
        inner_begin(total[64:80, :])
        full_r[mine64, :] = total[0:64, :]
        gather_r.start()
        ring.wait()
        total = ypc[p, own16, :]
        for d in range(1, 16):
            total = total + xr[p, d]
        full_c[own16, :] = total

        @pl.when(col == top)
        def _():
            top2[p, row, 0:16, :] = total[:, 0:B]
            top2[p, row, 16:32, :] = side_c[own16, 0:B]

        tops2.deal.start()
        gather_c.start()
        cholesky_block(aug, 1)
        inner_reduce()
        tops2.gather()
        cholesky_block(aug, 2)
        if p == 0:
            spread_e.forward()
        cholesky_block(aug, 3)

        upper = jnp.where(
            lax.broadcasted_iota(jnp.int32, (B, B), 1) >= lax.broadcasted_iota(jnp.int32, (B, B), 0), aug[:, 0:B], 0.0
        )
        band_ref[p] = upper / 128.0
        inverse = aug[:, B : 2 * B]
        tops1.ring.wait()
        c_t = dot(inverse, top1[p].reshape(B, B))
        power = c_t
        inverse_t = eye + power
        for _ in range(5):
            power = dot(power, power)
            inverse_t = inverse_t + dot(inverse_t, power)
        small[2] = inverse_t
        small[3] = dot(inverse, inverse_t, TN)

        def w_rows(m):
            rows = pl.ds(pl.multiple_of(m * B, B), B)
            left[rows, 0:B] = -dot(panel_r[rows, :], aug[:, B : 2 * B], NT)

        def w_cols(n):
            lanes = pl.ds(pl.multiple_of(n * B, B), B)
            right[B : 2 * B, lanes] = -dot(aug[:, B : 2 * B], panel_c[:, lanes])

        loop(0, 4, w_rows)
        loop(0, 4, w_cols)

        @pl.when(row == top)
        def _():
            left[0:B, 0:B] = left[0:B, 0:B] + eye

        @pl.when(col == top)
        def _():
            right[B : 2 * B, 0:B] = right[B : 2 * B, 0:B] + eye

        if p == 1:
            spread_e.forward()
        gather_r.forward()
        spread_e.wait()
        gather_r.wait()

        def u_rows(m):
            rows = pl.ds(pl.multiple_of(m * B, B), B)
            left[rows, B : 2 * B] = dot(side_r[rows, :], small[2]) - dot(full_r[rows, :], small[3])

        def u_cols(n):
            lanes = pl.ds(pl.multiple_of(n * B, B), B)
            right[0:B, lanes] = dot(small[2], side_c[:, lanes], TN) - dot(small[3], full_c[:, lanes], TN)

        loop(0, 4, u_rows)
        gather_c.wait()
        loop(0, 4, u_cols)

        inner_end()
        tops2.ring.wait()
        y_top = top2[p, :, 0:16, :].reshape(B, B)
        e_top = top2[p, :, 16:32, :].reshape(B, B)
        y_top = dot(inverse, y_top)
        x_top = e_top - y_top.T
        middle = x_top - y_top + dot(dot(inverse, sm2[p].reshape(B, B)), inverse, NT)
        half_sym = 0.5 * dot(inverse_t, dot(middle, inverse_t), TN)
        small[4] = half_sym

        def end_rows(m):
            rows = pl.ds(pl.multiple_of(m * B, B), B)
            left[rows, B : 2 * B] = left[rows, B : 2 * B] - dot(left[rows, 0:B], small[4])

        def end_cols(n):
            lanes = pl.ds(pl.multiple_of(n * B, B), B)
            right[0:B, lanes] = right[0:B, lanes] - dot(small[4], right[B : 2 * B, lanes], TN)

        loop(0, 4, end_rows)
        loop(0, 4, end_cols)
        if p == 1:
            return
        w_top_t = eye - c_t
        small[0] = w_top_t
        small[1] = dot(x_top, inverse_t) - dot(w_top_t, half_sym, TN)

        def next_rows(m):
            rows = pl.ds(pl.multiple_of(m * B, B), B)
            pr[1, rows, :] = (
                side_r[rows, :] - dot(left[rows, 0:B], small[1], NT) - dot(left[rows, B : 2 * B], small[0])
            )

        loop(0, 4, next_rows)

        @pl.when(row < 2)
        def _():
            pr[1, 0:B, :] = jnp.zeros((B, B), F32)

        def next_cols(n):
            lanes = pl.ds(pl.multiple_of(n * B, B), B)
            pc[1, :, lanes] = (
                side_c[:, lanes] - dot(small[1], right[B : 2 * B, lanes]) - dot(small[0], right[0:B, lanes], TN)
            )

        loop(0, 4, next_cols)

        @pl.when(col < 2)
        def _():
            pc[1, :, 0:B] = jnp.zeros((B, B), F32)

    class Tops:
        def __init__(self, source, slabs):
            own = slabs.at[row]
            self.deal = Deal(comm, col == source, at.col_peer, lambda t: own, lambda t: own, own)
            self.ring = Exchange(
                comm, 1, 16, at.row_peer, lambda d: own, lambda d: own, lambda d: slabs.at[at.row_from(d)]
            )

        def gather(self):
            self.deal.wait()
            self.ring.start()

    spread_p = Spread(0, pr.at[0], pc.at[0])
    spread_e = Spread(1, er.at[0], ec.at[0])
    tops_first = Tops(1, top1.at[0])
    spread_p.deal(True)
    spread_e.deal(False)
    spread_p.gather()

    @pl.when(col == 1)
    def _():
        top1[0, row] = pc[0, pl.ds(pl.multiple_of(16 * row, 16), 16), 0:B]

    tops_first.deal.start()
    spread_e.gather()
    tops_first.gather()
    spread_p.forward()
    spread_p.wait()
    first = comm.used
    panel(0, spread_e, tops_first)
    comm.finish()
    comm.used = 0
    spread_next = Spread(2, er.at[1], ec.at[1])
    tops_next = Tops(2, top1.at[1])
    comm.used = first
    panel(1, spread_next, tops_next)

    def last(n):
        lanes = pl.ds(pl.multiple_of(n * B, B), B)
        g[:, lanes] = g[:, lanes] - dot(left[...], right[:, lanes])

        @pl.when(row < 2)
        def _():
            g[0:B, lanes] = jnp.zeros((B, B), F32)

        @pl.when(jnp.logical_and(col < 2, n == 0))
        def _():
            g[:, lanes] = jnp.zeros((4 * B, B), F32)

        pltpu.make_async_copy(g.at[:, lanes], out_ref.at[:, lanes], local_sem.at[n]).start()

    loop(0, 4, last)
    comm.finish()

    def drain(n):
        lanes = pl.ds(pl.multiple_of(n * B, B), B)
        pltpu.make_async_copy(g.at[:, lanes], out_ref.at[:, lanes], local_sem.at[n]).wait()

    loop(0, 4, drain)


def shards(matrix_cyclic):
    vmem = lambda *shape: pltpu.VMEM(shape, F32)
    return pl.pallas_call(
        kernel,
        out_shape=(
            jax.ShapeDtypeStruct((1024, 1024), F32),
            jax.ShapeDtypeStruct((2, B, B), F32),
        ),
        in_specs=[pl.BlockSpec(memory_space=pl.ANY)],
        out_specs=(pl.BlockSpec(memory_space=pl.ANY), pl.BlockSpec(memory_space=pltpu.VMEM)),
        scratch_shapes=[
            vmem(1024, 1024),
            vmem(1024, B), vmem(B, 1024),
            vmem(2, 1024, B), vmem(2, B, 1024),
            vmem(2, 1024, B), vmem(2, B, 1024),
            vmem(B, 1024),
            vmem(2, 16, 80, B), vmem(2, B, 1024),
            vmem(2, 8, 80, B), vmem(2, 8, 80, B), vmem(2, 16, 16, 1024),
            vmem(2, 1024, B), vmem(2, B, 1024),
            vmem(2, 2, 16, 16, B), vmem(2, 16, 16, B), vmem(2, 16, 16, B),
            vmem(2, 16, 16, B), vmem(2, 16, 32, B),
            vmem(B, 2 * B),
            vmem(1024, 2 * B), vmem(2 * B, 1024),
            vmem(5, B, B),
            pltpu.SemaphoreType.DMA((4,)),
            pltpu.SemaphoreType.DMA((304,)),
            pltpu.SemaphoreType.DMA((304,)),
        ],
        compiler_params=pltpu.CompilerParams(
            collective_id=0, has_side_effects=True, vmem_limit_bytes=60 * 1024 * 1024
        ),
    )(matrix_cyclic)


def solution(mesh):
    return jax.shard_map(
        shards,
        mesh=mesh,
        in_specs=(P("row", "col"),),
        out_specs=(P("row", "col"), P()),
        check_vma=False,
    )
```

```python
import functools
import math

import jax
import jax.numpy as jnp
from jax import lax
from jax.experimental import pallas as pl
from jax.experimental.pallas import tpu as pltpu
from jax.sharding import PartitionSpec as P

B = 256
F32 = jnp.float32
HIGH = lax.Precision.HIGH
HIGHEST = lax.Precision.HIGHEST
NN = (((1,), (0,)), ((), ()))
NT = (((1,), (1,)), ((), ()))
TN = (((0,), (0,)), ((), ()))


def dot(left, right, dims=NN, precision=HIGH):
    return lax.dot_general(left, right, dims, precision=precision, preferred_element_type=F32)


class Place:
    def __init__(self):
        self.row = lax.axis_index("row")
        self.col = lax.axis_index("col")
        self.x, self.y = self.row // 4, lax.rem(self.row, 4)
        self.z, self.core = self.col // 2, lax.rem(self.col, 2)
        self.slot = self.core * 8 + self.z

    def z_peer(self, d):
        return (self.row, lax.rem(self.z + d, 8) * 2 + self.core)

    def z_slot_to(self, d):
        return self.core * 8 + lax.rem(self.z + d, 8)

    def z_slot_from(self, d):
        return self.core * 8 + lax.rem(self.z + 8 - d, 8)

    def sibling(self):
        return (self.row, self.col + 1 - 2 * self.core)

    def col_peer(self, t):
        return (self.row, lax.rem(self.col + t, 16))

    def col_slot_to(self, t):
        other = lax.rem(self.col + t, 16)
        return lax.rem(other, 2) * 8 + other // 2

    def row_peer(self, d):
        return (self.row_to(d), self.col)

    def row_to(self, d):
        return lax.rem(self.x + d // 4, 4) * 4 + lax.rem(self.y + lax.rem(d, 4), 4)

    def row_from(self, d):
        return lax.rem(self.x + 4 - d // 4, 4) * 4 + lax.rem(self.y + 4 - lax.rem(d, 4), 4)


def loop(start, stop, body):
    def step(i, carry):
        body(i)
        return carry

    lax.fori_loop(start, stop, step, 0)


class Comm:
    def __init__(self, place, send, recv):
        self.at = place
        self.send = send
        self.recv = recv
        self.used = 0
        self.sent = []

    def take(self, count):
        base = self.used
        self.used += count
        return base

    def copy(self, src, dst, send_index, recv_index, device):
        return pltpu.make_async_remote_copy(
            src_ref=src,
            dst_ref=dst,
            send_sem=self.send.at[send_index],
            recv_sem=self.recv.at[recv_index],
            device_id=device,
            device_id_type=pl.DeviceIdType.MESH,
        )

    def finish(self):
        for wait in self.sent:
            wait()
        self.sent = []


class Exchange:
    def __init__(self, comm, first, stop, peer, src, dst, landed):
        self.comm, self.first, self.stop = comm, first, stop
        self.peer, self.src, self.dst, self.landed = peer, src, dst, landed
        self.base = comm.take(stop - first) - first
        comm.sent.append(self.wait_sends)

    def start_one(self, d):
        i = self.base + d
        self.comm.copy(self.src(d), self.dst(d), i, i, self.peer(d)).start()

    def start(self):
        loop(self.first, self.stop, self.start_one)

    def wait_one(self, d):
        i = self.base + d
        self.comm.copy(self.landed(d), self.landed(d), i, i, self.peer(d)).wait_recv()

    def wait(self):
        loop(self.first, self.stop, self.wait_one)

    def wait_sends(self):
        def one(d):
            i = self.base + d
            self.comm.copy(self.src(d), self.dst(d), i, i, self.peer(d)).wait_send()

        loop(self.first, self.stop, one)


class Deal:
    def __init__(self, comm, source, peer, src, dst, landed):
        self.comm, self.source = comm, source
        self.peer, self.src, self.dst, self.landed = peer, src, dst, landed
        self.base = comm.take(16)
        comm.sent.append(self.wait_sends)

    def copy(self, t):
        return self.comm.copy(self.src(t), self.dst(t), self.base + t, self.base, self.peer(t))

    def start(self):
        @pl.when(self.source)
        def _():
            loop(1, 16, lambda t: self.copy(t).start())

    def wait(self):
        @pl.when(jnp.logical_not(self.source))
        def _():
            self.comm.copy(self.landed, self.landed, self.base, self.base, self.peer(1)).wait_recv()

    def wait_sends(self):
        @pl.when(self.source)
        def _():
            loop(1, 16, lambda t: self.copy(t).wait_send())


class GatherCol:
    def __init__(self, comm, part):
        at = comm.at
        self.at = at
        self.z = Exchange(
            comm, 1, 8, at.z_peer, lambda d: part(at.slot), lambda d: part(at.slot), lambda d: part(at.z_slot_from(d))
        )
        sibling = lambda d: at.sibling()
        other = lambda d: (1 - at.core) * 8 + lax.rem(at.z + 8 - d, 8)
        self.pair = Exchange(
            comm, 0, 8, sibling, lambda d: part(at.z_slot_from(d)), lambda d: part(at.z_slot_from(d)),
            lambda d: part(other(d)),
        )

    def start(self):
        self.z.start()
        self.pair.start_one(0)

    def forward(self):
        def one(d):
            self.z.wait_one(d)
            self.pair.start_one(d)

        loop(1, 8, one)

    def wait(self):
        self.pair.wait()


def cholesky_block(aug, block):
    sub = lax.broadcasted_iota(jnp.int32, (8, 128), 0)
    lane = lax.broadcasted_iota(jnp.int32, (8, 128), 1)
    base = 64 * block
    first = 128 * (base // 128)
    offset = base - first

    def strip(i):
        rows = pl.ds(pl.multiple_of(base + 8 * i, 8), 8)
        diag = pltpu.roll(aug[rows, first : first + 128], lax.rem(128 - offset - 8 * i, 128), 1)
        parts = [aug[rows, 128 * k : 128 * k + 128] for k in range(4)]
        cols = [jnp.broadcast_to(diag[:, j : j + 1], (8, 128)) for j in range(8)]
        pivots = jnp.ones((8, 128), F32)
        for j in range(8):
            pivot = jnp.broadcast_to(cols[j][j : j + 1, :], (8, 128))
            pivots = jnp.where(sub == j, pivot, pivots)
            scale = jnp.where(sub > j, cols[j] * (1.0 / pivot), 0.0)
            for k in range(j + 1, 8):
                cols[k] = cols[k] - scale * jnp.broadcast_to(cols[k][j : j + 1, :], (8, 128))
            for k in range(4):
                parts[k] = parts[k] - scale * jnp.broadcast_to(parts[k][j : j + 1, :], (8, 128))
        norm = 1.0 / jnp.sqrt(pivots)
        parts = [part * norm for part in parts]
        factors = jnp.where(lane >= offset + 8 * (i + 1), parts[first // 128], 0.0).T
        for t in range(8):
            below = slice(base + 8 * t, base + 8 * t + 8)
            spread = [
                jnp.broadcast_to(factors[offset + 8 * t : offset + 8 * t + 8, j : j + 1], (8, 128)) for j in range(8)
            ]
            for k in range(4):
                lanes = slice(128 * k, 128 * k + 128)
                rest = aug[below, lanes]
                for j in range(8):
                    rest = rest - spread[j] * jnp.broadcast_to(parts[k][j : j + 1, :], (8, 128))
                aug[below, lanes] = rest
        for k in range(4):
            aug[rows, 128 * k : 128 * k + 128] = parts[k]

    loop(0, 8, strip)
    if base + 64 < B:
        done = aug[base : base + 64, :]
        aug[base + 64 :, :] = aug[base + 64 :, :] - dot(done[:, base + 64 : B], done, TN, HIGHEST)


def kernel(a_ref, out_ref, band_ref, g, stage_r, stage_c, pr, pc, er, ec, prt, ypr, ypc, half, zr, xr, yr, yc,
           gx, sm1, sm2, top1, top2, aug, left, right, small, local_sem, send_sem, recv_sem):
    at = Place()
    comm = Comm(at, send_sem, recv_sem)
    row, col, slot = at.row, at.col, at.slot
    load = pltpu.make_async_copy(a_ref, g, local_sem.at[0])
    load.start()
    barrier = pltpu.get_barrier_semaphore()

    def greet(t):
        pl.semaphore_signal(barrier, inc=1, device_id=at.col_peer(t), device_id_type=pl.DeviceIdType.MESH)
        pl.semaphore_signal(barrier, inc=1, device_id=at.row_peer(t), device_id_type=pl.DeviceIdType.MESH)

    loop(1, 16, greet)
    load.wait()
    pl.semaphore_wait(barrier, 30)

    def rows64(ref, s):
        return ref.at[pl.ds(pl.multiple_of(64 * s, 64), 64)]

    def rows16(ref, s):
        return ref.at[pl.ds(pl.multiple_of(16 * s, 16), 16)]

    class Spread:
        def __init__(self, b, to_r, to_c):
            self.b, self.to_r, self.to_c = b, to_r, to_c
            self.deal_r = Deal(
                comm, col == b, at.col_peer,
                lambda t: rows64(stage_r, at.col_slot_to(t)), lambda t: rows64(to_r, at.col_slot_to(t)),
                rows64(to_r, slot),
            )
            self.deal_c = Deal(
                comm, row == b, at.row_peer,
                lambda t: rows16(stage_c, at.row_to(t)), lambda t: rows16(to_c, at.row_to(t)), rows16(to_c, row),
            )
            self.gather_r = GatherCol(comm, lambda s: rows64(to_r, s))
            self.gather_c = Exchange(
                comm, 1, 16, at.row_peer, lambda d: rows16(to_c, row), lambda d: rows16(to_c, row),
                lambda d: rows16(to_c, at.row_from(d)),
            )

        def deal(self, masked):
            @pl.when(col == self.b)
            def _():
                stage_r[...] = g[:, 0:B]
                if masked:
                    @pl.when(row == 0)
                    def _():
                        stage_r[0:B, :] = jnp.zeros((B, B), F32)
                mine = pl.ds(pl.multiple_of(64 * slot, 64), 64)
                self.to_r[mine, :] = stage_r[mine, :]

            self.deal_r.start()

            @pl.when(row == self.b)
            def _():
                stage_c[...] = g[0:B, :]
                if masked:
                    @pl.when(col == 0)
                    def _():
                        stage_c[:, 0:B] = jnp.zeros((B, B), F32)
                mine = pl.ds(pl.multiple_of(16 * row, 16), 16)
                self.to_c[mine, :] = stage_c[mine, :]

            self.deal_c.start()

        def gather(self):
            self.deal_r.wait()
            self.gather_r.start()
            self.deal_c.wait()
            self.gather_c.start()

        def forward(self):
            self.gather_r.forward()

        def wait(self):
            self.gather_r.wait()
            self.gather_c.wait()

    def panel(p, spread_e, tops1):
        panel_r, panel_c, side_r, side_c = pr.at[p], pc.at[p], er.at[p], ec.at[p]
        top = p + 1
        full_r, full_c = yr.at[p], yc.at[p]
        mine16 = pl.ds(pl.multiple_of(16 * slot, 16), 16)
        own16 = pl.ds(pl.multiple_of(16 * row, 16), 16)
        mine64 = pl.ds(pl.multiple_of(64 * slot, 64), 64)
        mine8 = pl.ds(pl.multiple_of(8 * at.core, 8), 8)

        def row_sum(which, sums):
            got = gx.at[p, which]
            ring = Exchange(comm, 1, 16, at.row_peer, lambda d: got.at[0], lambda d: got.at[d], lambda d: got.at[d])
            gather = GatherCol(comm, lambda s: sums.at[s])

            def begin(value):
                got[0] = value
                ring.start()

            def reduce():
                ring.wait()
                total = got[0]
                for d in range(1, 16):
                    total = total + got[d]
                sums[slot] = total
                gather.start()

            def end():
                gather.forward()
                gather.wait()

            return begin, reduce, end

        gram_begin, gram_reduce, gram_end = row_sum(0, sm1.at[p])
        inner_begin, inner_reduce, inner_end = row_sum(1, sm2.at[p])
        tops2 = Tops(top, top2.at[p])

        prt[...] = panel_r[...].T
        gram_begin(dot(prt[mine16, :], panel_r[...], NN, HIGHEST))

        if p == 1:
            @pl.when(col == top)
            def _():
                top1[p, row] = panel_c[own16, 0:B]

            tops1.deal.start()

            def update(n):
                lanes = pl.ds(pl.multiple_of(n * B, B), B)
                g[:, lanes] = g[:, lanes] - dot(left[...], right[:, lanes])

            loop(0, 4, update)
            spread_e.deal(False)

        pair = Exchange(
            comm, 0, 1, lambda d: at.sibling(),
            lambda d: ypr.at[p, pl.ds(pl.multiple_of(8 * (1 - at.core), 8), 8)], lambda d: half.at[p],
            lambda d: half.at[p],
        )
        cross = Exchange(
            comm, 1, 8, at.z_peer, lambda d: ypr.at[p, at.z_slot_to(d)], lambda d: zr.at[p, d], lambda d: zr.at[p, d]
        )
        ring = Exchange(
            comm, 1, 16, at.row_peer, lambda d: rows16(ypc.at[p], at.row_to(d)), lambda d: xr.at[p, d],
            lambda d: xr.at[p, d],
        )

        def product_rows(m):
            rows = pl.ds(pl.multiple_of(m * B, B), B)
            value = dot(g[rows, :], panel_c[...], NT)
            ypr[p, pl.ds(pl.multiple_of(4 * m, 4), 4), 0:64, :] = value.reshape(4, 64, B)

        def product_cols(n):
            lanes = pl.ds(pl.multiple_of(n * B, B), B)
            ypc[p, :, lanes] = dot(prt[...], g[:, lanes])

        loop(0, 4, product_rows)
        ypr[p, :, 64:80, :] = dot(prt[...], ypr[p, :, 0:64, :].reshape(4 * B, B)).reshape(16, 16, B)
        pair.start()
        loop(0, 2, product_cols)
        gram_reduce()
        pair.wait()
        ypr[p, mine8] = ypr[p, mine8] + half[p]
        cross.start()
        loop(2, 4, product_cols)
        ring.start()
        if p == 1:
            tops1.gather()
            spread_e.gather()

        gram_end()
        eye = (lax.broadcasted_iota(jnp.int32, (B, B), 0) == lax.broadcasted_iota(jnp.int32, (B, B), 1)).astype(F32)
        aug[:, 0:B] = sm1[p].reshape(B, B)
        aug[:, B : 2 * B] = eye
        cholesky_block(aug, 0)

        gather_r = GatherCol(comm, lambda s: rows64(full_r, s))
        gather_c = Exchange(
            comm, 1, 16, at.row_peer, lambda d: rows16(full_c, row), lambda d: rows16(full_c, row),
            lambda d: rows16(full_c, at.row_from(d)),
        )
        cross.wait()
        total = ypr[p, slot]
        for d in range(1, 8):
            total = total + zr[p, d]
        inner_begin(total[64:80, :])
        full_r[mine64, :] = total[0:64, :]
        gather_r.start()
        ring.wait()
        total = ypc[p, own16, :]
        for d in range(1, 16):
            total = total + xr[p, d]
        full_c[own16, :] = total

        @pl.when(col == top)
        def _():
            top2[p, row, 0:16, :] = total[:, 0:B]
            top2[p, row, 16:32, :] = side_c[own16, 0:B]

        tops2.deal.start()
        gather_c.start()
        cholesky_block(aug, 1)
        inner_reduce()
        tops2.gather()
        cholesky_block(aug, 2)
        if p == 0:
            spread_e.forward()
        cholesky_block(aug, 3)

        upper = jnp.where(
            lax.broadcasted_iota(jnp.int32, (B, B), 1) >= lax.broadcasted_iota(jnp.int32, (B, B), 0), aug[:, 0:B], 0.0
        )
        band_ref[p] = upper / 128.0
        inverse = aug[:, B : 2 * B]
        tops1.ring.wait()
        c_t = dot(inverse, top1[p].reshape(B, B))
        power = c_t
        inverse_t = eye + power
        for _ in range(5):
            power = dot(power, power)
            inverse_t = inverse_t + dot(inverse_t, power)
        small[2] = inverse_t
        small[3] = dot(inverse, inverse_t, TN)

        def w_rows(m):
            rows = pl.ds(pl.multiple_of(m * B, B), B)
            left[rows, 0:B] = -dot(panel_r[rows, :], aug[:, B : 2 * B], NT)

        def w_cols(n):
            lanes = pl.ds(pl.multiple_of(n * B, B), B)
            right[B : 2 * B, lanes] = -dot(aug[:, B : 2 * B], panel_c[:, lanes])

        loop(0, 4, w_rows)
        loop(0, 4, w_cols)

        @pl.when(row == top)
        def _():
            left[0:B, 0:B] = left[0:B, 0:B] + eye

        @pl.when(col == top)
        def _():
            right[B : 2 * B, 0:B] = right[B : 2 * B, 0:B] + eye

        if p == 1:
            spread_e.forward()
        gather_r.forward()
        spread_e.wait()
        gather_r.wait()

        def u_rows(m):
            rows = pl.ds(pl.multiple_of(m * B, B), B)
            left[rows, B : 2 * B] = dot(side_r[rows, :], small[2]) - dot(full_r[rows, :], small[3])

        def u_cols(n):
            lanes = pl.ds(pl.multiple_of(n * B, B), B)
            right[0:B, lanes] = dot(small[2], side_c[:, lanes], TN) - dot(small[3], full_c[:, lanes], TN)

        loop(0, 4, u_rows)
        gather_c.wait()
        loop(0, 4, u_cols)

        inner_end()
        tops2.ring.wait()
        y_top = top2[p, :, 0:16, :].reshape(B, B)
        e_top = top2[p, :, 16:32, :].reshape(B, B)
        y_top = dot(inverse, y_top)
        x_top = e_top - y_top.T
        middle = x_top - y_top + dot(dot(inverse, sm2[p].reshape(B, B)), inverse, NT)
        half_sym = 0.5 * dot(inverse_t, dot(middle, inverse_t), TN)
        small[4] = half_sym

        def end_rows(m):
            rows = pl.ds(pl.multiple_of(m * B, B), B)
            left[rows, B : 2 * B] = left[rows, B : 2 * B] - dot(left[rows, 0:B], small[4])

        def end_cols(n):
            lanes = pl.ds(pl.multiple_of(n * B, B), B)
            right[0:B, lanes] = right[0:B, lanes] - dot(small[4], right[B : 2 * B, lanes], TN)

        loop(0, 4, end_rows)
        loop(0, 4, end_cols)
        if p == 1:
            return
        w_top_t = eye - c_t
        small[0] = w_top_t
        small[1] = dot(x_top, inverse_t) - dot(w_top_t, half_sym, TN)

        def next_rows(m):
            rows = pl.ds(pl.multiple_of(m * B, B), B)
            pr[1, rows, :] = (
                side_r[rows, :] - dot(left[rows, 0:B], small[1], NT) - dot(left[rows, B : 2 * B], small[0])
            )

        loop(0, 4, next_rows)

        @pl.when(row < 2)
        def _():
            pr[1, 0:B, :] = jnp.zeros((B, B), F32)

        def next_cols(n):
            lanes = pl.ds(pl.multiple_of(n * B, B), B)
            pc[1, :, lanes] = (
                side_c[:, lanes] - dot(small[1], right[B : 2 * B, lanes]) - dot(small[0], right[0:B, lanes], TN)
            )

        loop(0, 4, next_cols)

        @pl.when(col < 2)
        def _():
            pc[1, :, 0:B] = jnp.zeros((B, B), F32)

    class Tops:
        def __init__(self, source, slabs):
            own = slabs.at[row]
            self.deal = Deal(comm, col == source, at.col_peer, lambda t: own, lambda t: own, own)
            self.ring = Exchange(
                comm, 1, 16, at.row_peer, lambda d: own, lambda d: own, lambda d: slabs.at[at.row_from(d)]
            )

        def gather(self):
            self.deal.wait()
            self.ring.start()

    spread_p = Spread(0, pr.at[0], pc.at[0])
    spread_e = Spread(1, er.at[0], ec.at[0])
    tops_first = Tops(1, top1.at[0])
    spread_p.deal(True)
    spread_p.gather()

    @pl.when(col == 1)
    def _():
        top1[0, row] = pc[0, pl.ds(pl.multiple_of(16 * row, 16), 16), 0:B]

    tops_first.deal.start()
    spread_e.deal(False)
    tops_first.gather()
    spread_p.forward()
    spread_e.gather()
    spread_p.wait()
    first = comm.used
    panel(0, spread_e, tops_first)
    comm.finish()
    comm.used = 0
    spread_next = Spread(2, er.at[1], ec.at[1])
    tops_next = Tops(2, top1.at[1])
    comm.used = first
    panel(1, spread_next, tops_next)

    def last(n):
        lanes = pl.ds(pl.multiple_of(n * B, B), B)
        g[:, lanes] = g[:, lanes] - dot(left[...], right[:, lanes])

        @pl.when(row < 2)
        def _():
            g[0:B, lanes] = jnp.zeros((B, B), F32)

        @pl.when(jnp.logical_and(col < 2, n == 0))
        def _():
            g[:, lanes] = jnp.zeros((4 * B, B), F32)

        pltpu.make_async_copy(g.at[:, lanes], out_ref.at[:, lanes], local_sem.at[n]).start()

    loop(0, 4, last)
    comm.finish()

    def drain(n):
        lanes = pl.ds(pl.multiple_of(n * B, B), B)
        pltpu.make_async_copy(g.at[:, lanes], out_ref.at[:, lanes], local_sem.at[n]).wait()

    loop(0, 4, drain)


def shards(matrix_cyclic):
    vmem = lambda *shape: pltpu.VMEM(shape, F32)
    return pl.pallas_call(
        kernel,
        out_shape=(
            jax.ShapeDtypeStruct((1024, 1024), F32),
            jax.ShapeDtypeStruct((2, B, B), F32),
        ),
        in_specs=[pl.BlockSpec(memory_space=pl.ANY)],
        out_specs=(pl.BlockSpec(memory_space=pl.ANY), pl.BlockSpec(memory_space=pltpu.VMEM)),
        scratch_shapes=[
            vmem(1024, 1024),
            vmem(1024, B), vmem(B, 1024),
            vmem(2, 1024, B), vmem(2, B, 1024),
            vmem(2, 1024, B), vmem(2, B, 1024),
            vmem(B, 1024),
            vmem(2, 16, 80, B), vmem(2, B, 1024),
            vmem(2, 8, 80, B), vmem(2, 8, 80, B), vmem(2, 16, 16, 1024),
            vmem(2, 1024, B), vmem(2, B, 1024),
            vmem(2, 2, 16, 16, B), vmem(2, 16, 16, B), vmem(2, 16, 16, B),
            vmem(2, 16, 16, B), vmem(2, 16, 32, B),
            vmem(B, 2 * B),
            vmem(1024, 2 * B), vmem(2 * B, 1024),
            vmem(5, B, B),
            pltpu.SemaphoreType.DMA((4,)),
            pltpu.SemaphoreType.DMA((304,)),
            pltpu.SemaphoreType.DMA((304,)),
        ],
        compiler_params=pltpu.CompilerParams(
            collective_id=0, has_side_effects=True, vmem_limit_bytes=60 * 1024 * 1024
        ),
    )(matrix_cyclic)


def solution(mesh):
    return jax.shard_map(
        shards,
        mesh=mesh,
        in_specs=(P("row", "col"),),
        out_specs=(P("row", "col"), P()),
        check_vma=False,
    )
```
